32 devices in a mesh: groups: 2 (over x), dp: 8 (over z, y), tensor: 2 (over core).
Axes of the slice: x: 2, y: 2, z: 4, core: 2. Of those that a mesh axis runs over, the one named last changes fastest.
Arguments:
- tokens: bfloat16 [16384, 8192], P(('groups', 'dp'), 'tensor'), parts along dimension 0, may hold values from -6 to 6
- base_weight: bfloat16 [8192, 1024], P('tensor', 'dp'), may hold values from -0.0625 to 0.0625
- adapt_a: bfloat16 [64, 32, 8192], P(('groups', 'dp'), None, 'tensor'), parts along dimension 0, may hold values from -0.0625 to 0.0625
- adapt_b: bfloat16 [64, 32, 1024], P(('groups', 'dp')), parts along dimension 0, may hold values from -1 to 1
- cotangent: bfloat16 [16384, 1024], P(('groups', 'dp'), 'tensor'), parts along dimension 0, may hold values from -6 to 6
- row_tenant: int32 [16384], P(('groups', 'dp')), parts along dimension 0, may hold values from 0 to 32, as said below
- adapter_slot: int32 [64], P('groups'), parts along dimension 0, may hold values from 0 to 31, as said below
Outputs:
- proj_out: bfloat16 [16384, 1024], P(('groups', 'dp'), 'tensor'), parts along dimension 0
- grad_a: bfloat16 [64, 32, 8192], P(('groups', 'dp'), None, 'tensor'), parts along dimension 0
- grad_b: bfloat16 [64, 32, 1024], P(('groups', 'dp'), None, 'tensor'), parts along dimension 0
The draws below stay inside these ranges and needn't reach their ends.
There are 2 independent parts, one for each index of `groups`. The reference program is written for one: setup_inputs(seed, part) draws one part's arguments, and reference() takes and returns one part's arrays. A program takes and returns all parts, laid end to end along the dimension named above; an argument that names none is the same for every part. Nothing has to cross between parts.
Inputs may be any that keep to these rules, and one draw needn't show every extreme that they name: `row_tenant`: each block of 128 rows holds one tenant's rows first (the first row always), then padding rows marked 32; the first block of every device uses an adapter on one common device, and the other blocks of a device use adapters on pairwise different devices other than that one. `adapter_slot`: A permutation of the slots.
All inputs are finite; a program needn't handle non-finite values.
Results may differ from the reference program's by a relative error of at most 0.0057.
Values may be sent and summed in bfloat16 or wider, within the bound.
No kernel may reach another device: no remote copies, remote signals or barrier semaphores. Data moves between devices by JAX's collectives and lax.ppermute only.
A program may use at most 128 MiB of HBM per device.

```python
import jax
import jax.numpy as jnp
from jax import lax

D = 8192
KV = 1024
R = 32
BLOCK = 128
TOK_DEV = 1024
TEN_DEV = 4
TOKENS = 8192
TENANTS = 32
N_DP = 8


def shared_slots(key):
    return jax.random.permutation(key, TENANTS).astype(jnp.int32)


def draw_adapter_slot(key, part):
    return shared_slots(key)


def draw_row_tenant(key, part):
    slots = shared_slots(key)
    key = jax.random.fold_in(key, 7)
    tenant_at = jnp.argsort(slots).astype(jnp.int32)
    count = TOK_DEV // BLOCK
    hottest = jax.random.randint(jax.random.fold_in(key, 1), (), 0, N_DP)

    def one_device(device):
        sub = jax.random.fold_in(key, 100 + device)
        offsets = jax.random.permutation(jax.random.fold_in(sub, 1), N_DP - 1)[:count - 1] + 1
        homes = jnp.concatenate([hottest[None], (hottest + offsets) % N_DP])
        local = jax.random.randint(jax.random.fold_in(sub, 2), (count,), 0, TEN_DEV)
        chosen = tenant_at[homes * TEN_DEV + local]
        filled = jax.random.randint(jax.random.fold_in(sub, 3), (count,), 1, BLOCK + 1)
        filled = filled.at[0].set(BLOCK)
        position = jnp.arange(BLOCK)
        layout = jnp.where(position[None, :] < filled[:, None], chosen[:, None], TENANTS)
        return layout.reshape(-1)
    return jax.vmap(one_device)(jnp.arange(N_DP)).reshape(-1).astype(jnp.int32)


def block_levels(stream_key, shape, cuts, low, largest):
    def one(axis_at, parts):
        steps = jax.random.uniform(jax.random.fold_in(jax.random.fold_in(stream_key, 6), axis_at), (parts,), jnp.float32, low / len(cuts), largest / len(cuts))
        return jnp.repeat(jnp.exp(steps), shape[axis_at] // parts).reshape((-1,) + (1,) * (len(shape) - axis_at - 1))

    loudness = one(*cuts[0])
    for cut in cuts[1:]:
        loudness = loudness * one(*cut)
    return loudness


def normal_values(key, extent, scale, limit, split=(), kind=jnp.bfloat16):
    loudness = block_levels(key, extent, split, -0.22, 0.18) if split else 1.0
    values = jax.random.normal(key, extent, jnp.float32) * scale * loudness
    return jnp.minimum(jnp.maximum(values, -limit), limit).astype(kind)


def setup_inputs(seed: int = 0, part: int = 0) -> dict:
    key_list = jax.random.split(jax.random.key(seed), 8)
    own_keys = jax.random.split(jax.random.fold_in(key_list[7], part), 8)
    return {
        "tokens": normal_values(own_keys[0], (TOKENS, D), 1.0, 6.0, ((0, 8), (1, 2))),
        "base_weight": normal_values(key_list[1], (D, KV), D ** -0.5, 0.0625, ((0, 2), (1, 8))),
        "adapt_a": normal_values(own_keys[2], (TENANTS, R, D), D ** -0.5, 0.0625, ((0, 8), (2, 2))),
        "adapt_b": normal_values(own_keys[3], (TENANTS, R, KV), R ** -0.5, 1.0, ((0, 8),)),
        "cotangent": normal_values(own_keys[4], (TOKENS, KV), 1.0, 6.0, ((0, 8), (1, 2))),
        "row_tenant": draw_row_tenant(jax.random.fold_in(jax.random.fold_in(key_list[7], part), 71), part),
        "adapter_slot": draw_adapter_slot(jax.random.fold_in(jax.random.fold_in(key_list[7], part), 71), part),
    }


ADAPTER_SCALING = 2.0


def reference(tokens, base_weight, adapt_a, adapt_b, cotangent, row_tenant, adapter_slot):
    blocks = TOKENS // BLOCK
    first = row_tenant.reshape(blocks, BLOCK)[:, 0]
    block_slot = adapter_slot[first].astype(jnp.int32)
    live = (row_tenant != TENANTS).reshape(blocks, BLOCK, 1)
    base = jnp.dot(tokens, base_weight, preferred_element_type=jnp.float32)
    token_tiles = tokens.reshape(blocks, BLOCK, D)
    grad_blocks = cotangent.reshape(blocks, BLOCK, KV)

    def per_block(items):
        rows_x, rows_dy, slot, alive = items
        down = adapt_a[slot]
        upmap = adapt_b[slot]
        hidden = jnp.dot(rows_x, down.T, preferred_element_type=jnp.float32)
        backward_pass = jnp.dot(rows_dy, upmap.T, preferred_element_type=jnp.float32)
        hidden = jnp.where(alive, hidden, 0.0).astype(jnp.bfloat16)
        backward_pass = jnp.where(alive, backward_pass, 0.0).astype(jnp.bfloat16)
        added = ADAPTER_SCALING * jnp.dot(hidden, upmap, preferred_element_type=jnp.float32)
        part_a = (ADAPTER_SCALING * jnp.dot(backward_pass.T, rows_x, preferred_element_type=jnp.float32)).astype(jnp.bfloat16)
        part_b = (ADAPTER_SCALING * jnp.dot(hidden.T, rows_dy, preferred_element_type=jnp.float32)).astype(jnp.bfloat16)
        return added, part_a, part_b

    added, part_a, part_b = lax.map(per_block, (token_tiles, grad_blocks, block_slot, live))
    proj_out = (base + added.reshape(TOKENS, KV)).astype(jnp.bfloat16)
    grad_a = jax.ops.segment_sum(part_a.astype(jnp.float32), block_slot, TENANTS).astype(jnp.bfloat16)
    grad_b = jax.ops.segment_sum(part_b.astype(jnp.float32), block_slot, TENANTS).astype(jnp.bfloat16)
    return proj_out, grad_a, grad_b
```

```python
import jax
import jax.numpy as jnp
from jax import lax
from jax.sharding import PartitionSpec as P

BLOCK = 128


ADAPTER_SCALING = 2.0
SWAP = [(0, 1), (1, 0)]


def dot(left, right, contract):
    return lax.dot_general(
        left, right, ((contract[0], contract[1]), ((), ())), preferred_element_type=jnp.float32
    )


def partial_base(tokens, base_weight):
    width = base_weight.shape[0]
    peers, core = lax.axis_size("dp"), lax.axis_index("tensor")
    if peers != 8 or lax.axis_size("groups") != 2:
        full = jnp.dot(
            tokens,
            lax.all_gather(base_weight, "dp", axis=1, tiled=True),
            preferred_element_type=jnp.float32,
        )
        mine = full.shape[1] // 2
        return (
            lax.dynamic_slice_in_dim(full, core * mine, mine, 1),
            lax.dynamic_slice_in_dim(full, (1 - core) * mine, mine, 1),
        )
    place, group = lax.axis_index("dp"), lax.axis_index("groups")
    layer, side = place // 2, place % 2
    pair = [(i, i ^ 2) for i in range(8)]
    middle = [(2, 4), (3, 5), (4, 2), (5, 3)]
    outward = [(2, 0), (3, 1), (4, 6), (5, 7)]
    across = [(i, i ^ 1) for i in range(8)]
    half = lax.dynamic_slice_in_dim(base_weight, group * (width // 2), width // 2, 0)
    near = lax.ppermute(half, "dp", pair)
    mid_next = lax.ppermute(half, "dp", middle)
    other_side = lax.ppermute(base_weight, "dp", across)
    mid_far = lax.ppermute(near, "dp", middle)
    end_next = lax.ppermute(mid_next, "dp", outward)
    end_far = lax.ppermute(mid_far, "dp", outward)
    inner = (layer == 1) | (layer == 2)
    halves = [near, jnp.where(inner, mid_next, end_next), jnp.where(inner, mid_far, end_far)]

    def whole(part):
        rest = lax.ppermute(part, "groups", SWAP)
        return jnp.where(
            group == 0, jnp.concatenate([part, rest], 0), jnp.concatenate([rest, part], 0)
        )

    def columns(part, part_across):
        return jnp.where(
            side == 0,
            jnp.concatenate([part, part_across], 1),
            jnp.concatenate([part_across, part], 1),
        )

    own = columns(base_weight, other_side)
    near, following, far = [
        columns(whole(part), whole(lax.ppermute(part, "dp", across))) for part in halves
    ]
    here = jnp.where(
        layer % 2 == 0, jnp.concatenate([own, near], 1), jnp.concatenate([near, own], 1)
    )
    there = jnp.where(
        layer < 2, jnp.concatenate([following, far], 1), jnp.concatenate([far, following], 1)
    )
    product_here = jnp.dot(tokens, here, preferred_element_type=jnp.float32)
    product_there = jnp.dot(tokens, there, preferred_element_type=jnp.float32)
    keep_here = layer // 2 == core
    return (
        jnp.where(keep_here, product_here, product_there),
        jnp.where(keep_here, product_there, product_here),
    )


def shards(tokens, base_weight, adapt_a, adapt_b, cotangent, row_tenant, adapter_slot):
    rows, half_width = tokens.shape
    ten_dev, rank, _ = adapt_a.shape
    output_columns = cotangent.shape[1]
    tenants_all = adapter_slot.shape[0]
    peers = lax.axis_size("dp")
    blocks = rows // BLOCK
    keep, give = partial_base(tokens, base_weight)
    first = row_tenant.reshape(blocks, BLOCK)[:, 0]
    table_ids = jnp.arange(tenants_all, dtype=jnp.int32)
    block_slot = jnp.sum(
        jnp.where(first[:, None] == table_ids[None, :], adapter_slot[None, :], 0), axis=1
    )
    block_home = block_slot // ten_dev
    block_local = block_slot % ten_dev
    peer_ids = jnp.arange(peers, dtype=jnp.int32)
    match = block_home[:, None] == peer_ids[None, :]
    wanted = ten_dev + jnp.sum(jnp.where(match, (block_local - ten_dev)[:, None], 0), axis=0)
    asked = lax.all_to_all(wanted.reshape(peers, 1), "dp", split_axis=0, concat_axis=0, tiled=True)
    asked_rows = jnp.broadcast_to(asked, (peers, rank)).reshape(peers * rank, 1)
    out_row = lax.broadcasted_iota(jnp.int32, (peers * rank, ten_dev * rank), 0)
    slot_row = lax.broadcasted_iota(jnp.int32, (peers * rank, ten_dev * rank), 1)
    select = (
        (asked_rows == slot_row // rank) & (out_row % rank == slot_row % rank)
    ).astype(jnp.bfloat16)
    column = lax.axis_index("tensor") * output_columns
    own_b = lax.dynamic_slice_in_dim(adapt_b, column, output_columns, 2)

    def to_peers(sent):
        return lax.all_to_all(
            sent.reshape(peers, rank, sent.shape[1]), "dp", split_axis=0, concat_axis=0, tiled=True
        ).reshape(sent.shape)

    def chosen(table):
        return dot(select, table.reshape(ten_dev * rank, -1), ((1,), (0,))).astype(jnp.bfloat16)

    got_b = to_peers(chosen(own_b))
    got_a = to_peers(chosen(adapt_a))
    row_home = jnp.broadcast_to(block_home[:, None], (blocks, BLOCK)).reshape(rows, 1)
    home_of = lax.broadcasted_iota(jnp.int32, (rows, peers * rank), 1) // rank
    counted = (row_home == home_of) & (row_tenant != tenants_all)[:, None]

    def rank_space(part):
        total = part + lax.ppermute(part, "tensor", SWAP)
        return jnp.where(counted, total, 0.0).astype(jnp.bfloat16)

    backward_pass = rank_space(dot(cotangent, got_b, ((1,), (1,))))
    home_a = (ADAPTER_SCALING * dot(backward_pass, tokens, ((0,), (0,)))).astype(jnp.bfloat16)
    came_a = to_peers(home_a)
    hidden = rank_space(dot(tokens, got_a, ((1,), (1,))))
    home_b = (ADAPTER_SCALING * dot(hidden, cotangent, ((0,), (0,)))).astype(jnp.bfloat16)
    came_b = to_peers(home_b)
    added = ADAPTER_SCALING * dot(hidden, got_b, ((1,), (0,)))
    base = keep + lax.ppermute(give, "tensor", SWAP)
    proj_out = (base + added).astype(jnp.bfloat16)
    total_a = dot(select, came_a, ((0,), (0,))).astype(jnp.bfloat16)
    total_b = dot(select, came_b, ((0,), (0,))).astype(jnp.bfloat16)
    return (
        proj_out,
        total_a.reshape(ten_dev, rank, half_width),
        total_b.reshape(ten_dev, rank, output_columns),
    )


def solution(mesh):
    return jax.shard_map(
        shards,
        mesh=mesh,
        in_specs=(
            P(("groups", "dp"), "tensor"),
            P("tensor", "dp"),
            P(("groups", "dp"), None, "tensor"),
            P(("groups", "dp"), None, None),
            P(("groups", "dp"), "tensor"),
            P(("groups", "dp")),
            P("groups"),
        ),
        out_specs=(
            P(("groups", "dp"), "tensor"),
            P(("groups", "dp"), None, "tensor"),
            P(("groups", "dp"), None, "tensor"),
        ),
        check_vma=False,
    )
```

```python
import jax
import jax.numpy as jnp
from jax import lax
from jax.sharding import PartitionSpec as P

BLOCK = 128


ADAPTER_SCALING = 2.0
SWAP = [(0, 1), (1, 0)]


def dot(left, right, contract):
    return lax.dot_general(
        left, right, ((contract[0], contract[1]), ((), ())), preferred_element_type=jnp.float32
    )


def after(value, *others):
    return lax.optimization_barrier((value, *others))[0]


def in_order(group, part, rest):
    return jnp.where(
        group == 0, jnp.concatenate([part, rest], 0), jnp.concatenate([rest, part], 0)
    )


def beside(side, part, other):
    return jnp.where(
        side == 0, jnp.concatenate([part, other], 1), jnp.concatenate([other, part], 1)
    )


class Adapters:
    def __init__(self, tokens, adapt_a, adapt_b, cotangent, row_tenant, adapter_slot):
        self.tokens, self.cotangent = tokens, cotangent
        self.rows = tokens.shape[0]
        self.ten_dev, self.rank, _ = adapt_a.shape
        self.peers, self.place = lax.axis_size("dp"), lax.axis_index("dp")
        tenants_all, blocks = adapter_slot.shape[0], self.rows // BLOCK
        first = row_tenant.reshape(blocks, BLOCK)[:, 0]
        table_ids = jnp.arange(tenants_all, dtype=jnp.int32)
        block_slot = jnp.sum(
            jnp.where(first[:, None] == table_ids[None, :], adapter_slot[None, :], 0), axis=1
        )
        block_home = block_slot // self.ten_dev
        block_local = block_slot % self.ten_dev
        peer_ids = jnp.arange(self.peers, dtype=jnp.int32)
        match = block_home[:, None] == peer_ids[None, :]
        self.wanted = self.ten_dev + jnp.sum(
            jnp.where(match, (block_local - self.ten_dev)[:, None], 0), axis=0
        )
        columns = self.peers * self.rank
        row_home = jnp.broadcast_to(block_home[:, None], (blocks, BLOCK)).reshape(-1, 1)
        home_of = lax.broadcasted_iota(jnp.int32, (self.rows, columns), 1) // self.rank
        self.counted = (row_home == home_of) & (row_tenant != tenants_all)[:, None]
        output_columns = cotangent.shape[1]
        column = lax.axis_index("tensor") * output_columns
        self.own_a = adapt_a
        self.own_b = lax.dynamic_slice_in_dim(adapt_b, column, output_columns, 2)

    def exchange(self, sent):
        return lax.all_to_all(
            sent.reshape(self.peers, -1, sent.shape[1]), "dp", split_axis=0, concat_axis=0, tiled=True
        ).reshape(sent.shape)

    def choose(self, asked):
        asked_rows = jnp.broadcast_to(asked, (self.peers, self.rank)).reshape(-1, 1)
        shape = (self.peers * self.rank, self.ten_dev * self.rank)
        out_row = lax.broadcasted_iota(jnp.int32, shape, 0)
        slot_row = lax.broadcasted_iota(jnp.int32, shape, 1)
        self.select = (
            (asked_rows == slot_row // self.rank) & (out_row % self.rank == slot_row % self.rank)
        ).astype(jnp.bfloat16)

    def chosen(self, table):
        return dot(
            self.select, table.reshape(self.ten_dev * self.rank, -1), ((1,), (0,))
        ).astype(jnp.bfloat16)

    def rank_space(self, part):
        total = part + lax.ppermute(part, "tensor", SWAP)
        return jnp.where(self.counted, total, 0.0).astype(jnp.bfloat16)

    def term(self, left, right):
        return (ADAPTER_SCALING * dot(left, right, ((0,), (0,)))).astype(jnp.bfloat16)

    def total(self, came):
        return (
            dot(self.select, came, ((0,), (0,)))
            .astype(jnp.bfloat16)
            .reshape(self.ten_dev, self.rank, -1)
        )


def plain(tokens, base_weight, adapters):
    adapters.choose(adapters.exchange(adapters.wanted.reshape(-1, 1)))
    full = jnp.dot(
        tokens,
        lax.all_gather(base_weight, "dp", axis=1, tiled=True),
        preferred_element_type=jnp.float32,
    )
    base = lax.psum_scatter(full, "tensor", scatter_dimension=1, tiled=True)
    got_b = adapters.exchange(adapters.chosen(adapters.own_b))
    got_a = adapters.exchange(adapters.chosen(adapters.own_a))
    backward_pass = adapters.rank_space(dot(adapters.cotangent, got_b, ((1,), (1,))))
    came_a = adapters.exchange(adapters.term(backward_pass, tokens))
    hidden = adapters.rank_space(dot(tokens, got_a, ((1,), (1,))))
    came_b = adapters.exchange(adapters.term(hidden, adapters.cotangent))
    added = ADAPTER_SCALING * dot(hidden, got_b, ((1,), (0,)))
    return (
        (base + added).astype(jnp.bfloat16),
        adapters.total(came_a),
        adapters.total(came_b),
    )


def shards(tokens, base_weight, adapt_a, adapt_b, cotangent, row_tenant, adapter_slot):
    work = Adapters(tokens, adapt_a, adapt_b, cotangent, row_tenant, adapter_slot)
    if lax.axis_size("dp") != 8 or lax.axis_size("groups") != 2:
        return plain(tokens, base_weight, work)
    width = base_weight.shape[0]
    place, group, core = lax.axis_index("dp"), lax.axis_index("groups"), lax.axis_index("tensor")
    layer, side = place // 2, place % 2
    inner = (layer == 1) | (layer == 2)
    pair = [(i, i ^ 2) for i in range(8)]
    middle = [(2, 4), (3, 5), (4, 2), (5, 3)]
    outward = [(2, 0), (3, 1), (4, 6), (5, 7)]
    across = [(i, i ^ 1) for i in range(8)]

    def over(part, pairs):
        return lax.ppermute(part, "dp", pairs)

    def twin(part):
        return lax.ppermute(part, "groups", SWAP)

    barrier = lax.optimization_barrier
    half = lax.dynamic_slice_in_dim(base_weight, group * (width // 2), width // 2, 0)
    near = over(half, pair)
    mid_next = over(half, middle)
    own_across = over(half, across)
    asked = work.exchange(work.wanted.reshape(-1, 1))
    near, mid_next, own_across, asked = barrier((near, mid_next, own_across, asked))
    mid_far = over(near, middle)
    end_next = over(mid_next, outward)
    near_across = over(near, across)
    near_rest = twin(near)
    own_across_rest = twin(own_across)
    work.choose(asked)
    got_b = work.exchange(work.chosen(work.own_b))
    send_a = work.chosen(work.own_a)
    mid_far, end_next, near_across, near_rest, own_across_rest, got_b, send_a = barrier(
        (mid_far, end_next, near_across, near_rest, own_across_rest, got_b, send_a)
    )
    got_a = work.exchange(send_a)
    end_far = over(mid_far, outward)
    following = jnp.where(inner, mid_next, end_next)
    following_across = over(following, across)
    following_rest = twin(following)
    near_across_rest = twin(near_across)
    backward_pass = work.rank_space(dot(cotangent, got_b, ((1,), (1,))))
    home_a = work.term(backward_pass, tokens)
    own = beside(side, base_weight, in_order(group, own_across, own_across_rest))
    got_a, home_a, end_far, following_across, following_rest, near_across_rest, own = barrier(
        (got_a, home_a, end_far, following_across, following_rest, near_across_rest, own)
    )
    came_a = work.exchange(home_a)
    far = jnp.where(inner, mid_far, end_far)
    far_across = over(far, across)
    far_rest = twin(far)
    following_across_rest = twin(following_across)
    far_across_rest = twin(far_across)
    near = beside(
        side, in_order(group, near, near_rest), in_order(group, near_across, near_across_rest)
    )
    here = jnp.where(
        layer % 2 == 0, jnp.concatenate([own, near], 1), jnp.concatenate([near, own], 1)
    )
    product_here = jnp.dot(tokens, here, preferred_element_type=jnp.float32)
    hidden = work.rank_space(dot(tokens, got_a, ((1,), (1,))))
    home_b = work.term(hidden, cotangent)
    added = ADAPTER_SCALING * dot(hidden, got_b, ((1,), (0,)))
    following = beside(
        side,
        in_order(group, following, following_rest),
        in_order(group, following_across, following_across_rest),
    )
    far = beside(side, in_order(group, far, far_rest), in_order(group, far_across, far_across_rest))
    there = jnp.where(
        layer < 2, jnp.concatenate([following, far], 1), jnp.concatenate([far, following], 1)
    )
    product_there = jnp.dot(tokens, there, preferred_element_type=jnp.float32)
    keep_here = layer // 2 == core
    keep = jnp.where(keep_here, product_here, product_there)
    give = jnp.where(keep_here, product_there, product_here)
    base = keep + lax.ppermute(give, "tensor", SWAP)
    proj_out = (base + added).astype(jnp.bfloat16)
    came_a, home_b, proj_out = barrier((came_a, home_b, proj_out))
    came_b = work.exchange(home_b)
    return proj_out, work.total(came_a), work.total(came_b)


def solution(mesh):
    return jax.shard_map(
        shards,
        mesh=mesh,
        in_specs=(
            P(("groups", "dp"), "tensor"),
            P("tensor", "dp"),
            P(("groups", "dp"), None, "tensor"),
            P(("groups", "dp"), None, None),
            P(("groups", "dp"), "tensor"),
            P(("groups", "dp")),
            P("groups"),
        ),
        out_specs=(
            P(("groups", "dp"), "tensor"),
            P(("groups", "dp"), None, "tensor"),
            P(("groups", "dp"), None, "tensor"),
        ),
        check_vma=False,
    )
```

```python
import functools

import jax
import jax.numpy as jnp
from jax import lax
from jax.experimental import pallas as pl
from jax.experimental.pallas import tpu as pltpu
from jax.sharding import PartitionSpec as P

BLOCK = 128


ADAPTER_SCALING = 2.0
SWAP = [(0, 1), (1, 0)]


def dot(left, right, contract):
    return lax.dot_general(
        left, right, ((contract[0], contract[1]), ((), ())), preferred_element_type=jnp.float32
    )


LITTLE = pl.CostEstimate(flops=1_000_000, bytes_accessed=10_000, transcendentals=0)


def cost(rows, depth, columns):
    return pl.CostEstimate(
        flops=2 * rows * depth * columns, bytes_accessed=2 * rows * depth, transcendentals=0
    )


VMEM_BYTES = 40 * 1024 * 1024


def product_kernel(count, place_ref, tokens_ref, *refs):
    pieces, out_ref, weight, sems = refs[:count], refs[count], refs[count + 1], refs[count + 2]

    @pl.when(pl.program_id(0) == 0)
    def _():
        copies = []
        for k, piece in enumerate(pieces):
            depth = piece.shape[0]
            row = pl.multiple_of(place_ref[2 * k] * depth, depth)
            column = pl.multiple_of(place_ref[2 * k + 1] * piece.shape[1], piece.shape[1])
            copies.append(
                pltpu.make_async_copy(
                    piece,
                    weight.at[pl.ds(row, depth), pl.ds(column, piece.shape[1])],
                    sems.at[k],
                )
            )
        for copy in copies:
            copy.start()
        for copy in copies:
            copy.wait()

    out_ref[...] = jnp.dot(tokens_ref[...], weight[...], preferred_element_type=jnp.float32)


def product(tokens, pieces, places, width, estimate):
    rows, depth = tokens.shape
    tile = rows // 4
    return pl.pallas_call(
        functools.partial(product_kernel, len(pieces)),
        out_shape=jax.ShapeDtypeStruct((rows, width), jnp.float32),
        grid_spec=pltpu.PrefetchScalarGridSpec(
            num_scalar_prefetch=1,
            grid=(rows // tile,),
            in_specs=[pl.BlockSpec((tile, depth), lambda i, place: (i, 0))]
            + [pl.BlockSpec(memory_space=pl.ANY)] * len(pieces),
            out_specs=pl.BlockSpec((tile, width), lambda i, place: (i, 0)),
            scratch_shapes=[
                pltpu.VMEM((depth, width), jnp.bfloat16),
                pltpu.SemaphoreType.DMA((len(pieces),)),
            ],
        ),
        compiler_params=pltpu.CompilerParams(vmem_limit_bytes=VMEM_BYTES),
        cost_estimate=estimate,
        name="weight_product",
    )(jnp.stack([jnp.int32(v) for place in places for v in place]), tokens, *pieces)


def hidden_kernel(maps_ref, tokens_ref, out_ref):
    out_ref[...] = dot(maps_ref[...], tokens_ref[...], ((1,), (1,)))


def hidden_product(maps, tokens):
    rows, depth = tokens.shape
    tile = rows // 4
    return pl.pallas_call(
        hidden_kernel,
        out_shape=jax.ShapeDtypeStruct((maps.shape[0], rows), jnp.float32),
        grid=(rows // tile,),
        in_specs=[
            pl.BlockSpec(maps.shape, lambda i: (0, 0)),
            pl.BlockSpec((tile, depth), lambda i: (i, 0)),
        ],
        out_specs=pl.BlockSpec((maps.shape[0], tile), lambda i: (0, i)),
        compiler_params=pltpu.CompilerParams(vmem_limit_bytes=VMEM_BYTES),
        cost_estimate=LITTLE,
        name="hidden_product",
    )(maps, tokens)


def term_kernel(space_ref, tokens_ref, out_ref):
    total = jnp.dot(space_ref[...], tokens_ref[...], preferred_element_type=jnp.float32)
    out_ref[...] = (ADAPTER_SCALING * total).astype(jnp.bfloat16)


def gradient_term(space, values):
    rows, depth = values.shape
    tile = depth // 8
    return pl.pallas_call(
        term_kernel,
        out_shape=jax.ShapeDtypeStruct((space.shape[0], depth), jnp.bfloat16),
        grid=(depth // tile,),
        in_specs=[
            pl.BlockSpec(space.shape, lambda i: (0, 0)),
            pl.BlockSpec((rows, tile), lambda i: (0, i)),
        ],
        out_specs=pl.BlockSpec((space.shape[0], tile), lambda i: (0, i)),
        compiler_params=pltpu.CompilerParams(vmem_limit_bytes=VMEM_BYTES),
        cost_estimate=LITTLE,
        name="gradient_term",
    )(space, values)


class Adapters:
    def __init__(self, tokens, adapt_a, adapt_b, cotangent, row_tenant, adapter_slot):
        self.tokens, self.cotangent = tokens, cotangent
        self.rows = tokens.shape[0]
        self.ten_dev, self.rank, _ = adapt_a.shape
        self.peers, self.place = lax.axis_size("dp"), lax.axis_index("dp")
        tenants_all, blocks = adapter_slot.shape[0], self.rows // BLOCK
        first = row_tenant.reshape(blocks, BLOCK)[:, 0]
        table_ids = jnp.arange(tenants_all, dtype=jnp.int32)
        block_slot = jnp.sum(
            jnp.where(first[:, None] == table_ids[None, :], adapter_slot[None, :], 0), axis=1
        )
        block_home = block_slot // self.ten_dev
        block_local = block_slot % self.ten_dev
        peer_ids = jnp.arange(self.peers, dtype=jnp.int32)
        match = block_home[:, None] == peer_ids[None, :]
        self.wanted = self.ten_dev + jnp.sum(
            jnp.where(match, (block_local - self.ten_dev)[:, None], 0), axis=0
        )
        columns = self.peers * self.rank
        row_home = jnp.broadcast_to(block_home[:, None], (blocks, BLOCK)).reshape(1, -1)
        home_of = lax.broadcasted_iota(jnp.int32, (columns, self.rows), 0) // self.rank
        self.counted = (row_home == home_of) & (row_tenant != tenants_all)[None, :]
        output_columns = cotangent.shape[1]
        column = lax.axis_index("tensor") * output_columns
        self.own_a = adapt_a
        self.own_b = lax.dynamic_slice_in_dim(adapt_b, column, output_columns, 2)

    def exchange(self, sent):
        return lax.all_to_all(
            sent.reshape(self.peers, -1, sent.shape[1]), "dp", split_axis=0, concat_axis=0, tiled=True
        ).reshape(sent.shape)

    def choose(self, asked):
        asked_rows = jnp.broadcast_to(asked, (self.peers, self.rank)).reshape(-1, 1)
        shape = (self.peers * self.rank, self.ten_dev * self.rank)
        out_row = lax.broadcasted_iota(jnp.int32, shape, 0)
        slot_row = lax.broadcasted_iota(jnp.int32, shape, 1)
        self.select = (
            (asked_rows == slot_row // self.rank) & (out_row % self.rank == slot_row % self.rank)
        ).astype(jnp.bfloat16)

    def chosen(self, table):
        return dot(
            self.select, table.reshape(self.ten_dev * self.rank, -1), ((1,), (0,))
        ).astype(jnp.bfloat16)

    def rank_space(self, part):
        total = part + lax.ppermute(part, "tensor", SWAP)
        return jnp.where(self.counted, total, 0.0).astype(jnp.bfloat16)

    def term(self, space, values):
        return (ADAPTER_SCALING * dot(space, values, ((1,), (0,)))).astype(jnp.bfloat16)

    def total(self, came):
        return (
            dot(self.select, came, ((0,), (0,)))
            .astype(jnp.bfloat16)
            .reshape(self.ten_dev, self.rank, -1)
        )


def plain(tokens, base_weight, adapters):
    adapters.choose(adapters.exchange(adapters.wanted.reshape(-1, 1)))
    full = jnp.dot(
        tokens,
        lax.all_gather(base_weight, "dp", axis=1, tiled=True),
        preferred_element_type=jnp.float32,
    )
    base = lax.psum_scatter(full, "tensor", scatter_dimension=1, tiled=True)
    got_b = adapters.exchange(adapters.chosen(adapters.own_b))
    got_a = adapters.exchange(adapters.chosen(adapters.own_a))
    backward_pass = adapters.rank_space(dot(got_b, adapters.cotangent, ((1,), (1,))))
    came_a = adapters.exchange(adapters.term(backward_pass, tokens))
    hidden = adapters.rank_space(dot(got_a, tokens, ((1,), (1,))))
    came_b = adapters.exchange(adapters.term(hidden, adapters.cotangent))
    added = ADAPTER_SCALING * dot(hidden, got_b, ((0,), (0,)))
    return (
        (base + added).astype(jnp.bfloat16),
        adapters.total(came_a),
        adapters.total(came_b),
    )


def shards(tokens, base_weight, adapt_a, adapt_b, cotangent, row_tenant, adapter_slot):
    work = Adapters(tokens, adapt_a, adapt_b, cotangent, row_tenant, adapter_slot)
    if lax.axis_size("dp") != 8 or lax.axis_size("groups") != 2:
        return plain(tokens, base_weight, work)
    width = base_weight.shape[0]
    place, group, core = lax.axis_index("dp"), lax.axis_index("groups"), lax.axis_index("tensor")
    layer, side = place // 2, place % 2
    inner = (layer == 1) | (layer == 2)
    pair = [(i, i ^ 2) for i in range(8)]
    middle = [(2, 4), (3, 5), (4, 2), (5, 3)]
    outward = [(2, 0), (3, 1), (4, 6), (5, 7)]
    across = [(i, i ^ 1) for i in range(8)]

    def over(part, pairs):
        return lax.ppermute(part, "dp", pairs)

    def twin(part):
        return lax.ppermute(part, "groups", SWAP)

    output_columns = cotangent.shape[1]
    barrier = lax.optimization_barrier

    half = lax.dynamic_slice_in_dim(base_weight, group * (width // 2), width // 2, 0)
    near = over(half, pair)
    mid_next = over(half, middle)
    own_across = over(half, across)
    asked = work.exchange(work.wanted.reshape(-1, 1))
    near, mid_next, own_across, asked = barrier((near, mid_next, own_across, asked))
    mid_far = over(near, middle)
    end_next = over(mid_next, outward)
    near_across = over(near, across)
    near_rest = twin(near)
    own_across_rest = twin(own_across)
    work.choose(asked)
    got_b = work.exchange(work.chosen(work.own_b))
    send_a = work.chosen(work.own_a)
    mid_far, end_next, near_across, near_rest, own_across_rest, got_b, send_a = barrier(
        (mid_far, end_next, near_across, near_rest, own_across_rest, got_b, send_a)
    )
    got_a = work.exchange(send_a)
    end_far = over(mid_far, outward)
    following = jnp.where(inner, mid_next, end_next)
    following_across = over(following, across)
    following_rest = twin(following)
    near_across_rest = twin(near_across)
    backward_pass = work.rank_space(dot(got_b, cotangent, ((1,), (1,))))
    home_a = gradient_term(backward_pass, tokens)
    following_across_rest = twin(following_across)
    end_far, home_a = barrier((end_far, home_a))
    far = jnp.where(inner, mid_far, end_far)
    (
        got_a,
        home_a,
        far,
        following_across,
        following_rest,
        following_across_rest,
        near_across_rest,
    ) = barrier(
        (
            got_a,
            home_a,
            far,
            following_across,
            following_rest,
            following_across_rest,
            near_across_rest,
        )
    )
    came_a = work.exchange(home_a)
    far_across = over(far, across)
    far_rest = twin(far)
    parity = layer % 2
    product_here = product(
        tokens,
        [
            base_weight,
            own_across,
            own_across_rest,
            near,
            near_rest,
            near_across,
            near_across_rest,
        ],
        [
            (0, 2 * parity + side),
            (group, 2 * parity + 1 - side),
            (1 - group, 2 * parity + 1 - side),
            (group, 2 * (1 - parity) + side),
            (1 - group, 2 * (1 - parity) + side),
            (group, 2 * (1 - parity) + 1 - side),
            (1 - group, 2 * (1 - parity) + 1 - side),
        ],
        output_columns,
        cost(*tokens.shape, output_columns),
    )
    got_a, product_here, far_rest, far_across = barrier(
        (got_a, product_here, far_rest, far_across)
    )
    far_across_rest = twin(far_across)
    halves = [
        product(
            tokens,
            list(pieces),
            [(row, column) for column in (side, 1 - side) for row in (group, 1 - group)],
            output_columns // 2,
            LITTLE,
        )
        for pieces in (
            (following, following_rest, following_across, following_across_rest),
            (far, far_rest, far_across, far_across_rest),
        )
    ]
    product_there = jnp.where(
        layer < 2, jnp.concatenate(halves, 1), jnp.concatenate(halves[::-1], 1)
    )
    hidden = work.rank_space(hidden_product(got_a, tokens))
    home_b = work.term(hidden, cotangent)
    added = ADAPTER_SCALING * dot(hidden, got_b, ((0,), (0,)))
    keep_here = layer // 2 == core
    keep = jnp.where(keep_here, product_here, product_there)
    give = jnp.where(keep_here, product_there, product_here)
    base = keep + lax.ppermute(give, "tensor", SWAP)
    proj_out = (base + added).astype(jnp.bfloat16)
    came_a, home_b, proj_out = barrier((came_a, home_b, proj_out))
    came_b = work.exchange(home_b)
    return proj_out, work.total(came_a), work.total(came_b)


def solution(mesh):
    return jax.shard_map(
        shards,
        mesh=mesh,
        in_specs=(
            P(("groups", "dp"), "tensor"),
            P("tensor", "dp"),
            P(("groups", "dp"), None, "tensor"),
            P(("groups", "dp"), None, None),
            P(("groups", "dp"), "tensor"),
            P(("groups", "dp")),
            P("groups"),
        ),
        out_specs=(
            P(("groups", "dp"), "tensor"),
            P(("groups", "dp"), None, "tensor"),
            P(("groups", "dp"), None, "tensor"),
        ),
        check_vma=False,
    )
```

```python
import functools

import jax
import jax.numpy as jnp
from jax import lax
from jax.experimental import pallas as pl
from jax.experimental.pallas import tpu as pltpu
from jax.sharding import PartitionSpec as P

BLOCK = 128


ADAPTER_SCALING = 2.0
SWAP = [(0, 1), (1, 0)]


def dot(left, right, contract):
    return lax.dot_general(
        left, right, ((contract[0], contract[1]), ((), ())), preferred_element_type=jnp.float32
    )


LITTLE = pl.CostEstimate(flops=1_000_000, bytes_accessed=10_000, transcendentals=0)


def cost(rows, depth, columns):
    return pl.CostEstimate(
        flops=2 * rows * depth * columns, bytes_accessed=2 * rows * depth, transcendentals=0
    )


VMEM_BYTES = 40 * 1024 * 1024


def product_kernel(count, place_ref, tokens_ref, *refs):
    pieces, out_ref, weight, sems = refs[:count], refs[count], refs[count + 1], refs[count + 2]

    @pl.when(pl.program_id(0) == 0)
    def _():
        copies = []
        for k, piece in enumerate(pieces):
            depth = piece.shape[0]
            row = pl.multiple_of(place_ref[2 * k] * depth, depth)
            column = pl.multiple_of(place_ref[2 * k + 1] * piece.shape[1], piece.shape[1])
            copies.append(
                pltpu.make_async_copy(
                    piece,
                    weight.at[pl.ds(row, depth), pl.ds(column, piece.shape[1])],
                    sems.at[k],
                )
            )
        for copy in copies:
            copy.start()
        for copy in copies:
            copy.wait()

    out_ref[...] = jnp.dot(tokens_ref[...], weight[...], preferred_element_type=jnp.float32)


def product(tokens, pieces, places, width, estimate):
    rows, depth = tokens.shape
    tile = rows // 4
    return pl.pallas_call(
        functools.partial(product_kernel, len(pieces)),
        out_shape=jax.ShapeDtypeStruct((rows, width), jnp.float32),
        grid_spec=pltpu.PrefetchScalarGridSpec(
            num_scalar_prefetch=1,
            grid=(rows // tile,),
            in_specs=[pl.BlockSpec((tile, depth), lambda i, place: (i, 0))]
            + [pl.BlockSpec(memory_space=pl.ANY)] * len(pieces),
            out_specs=pl.BlockSpec((tile, width), lambda i, place: (i, 0)),
            scratch_shapes=[
                pltpu.VMEM((depth, width), jnp.bfloat16),
                pltpu.SemaphoreType.DMA((len(pieces),)),
            ],
        ),
        compiler_params=pltpu.CompilerParams(vmem_limit_bytes=VMEM_BYTES),
        cost_estimate=estimate,
        name="weight_product",
    )(jnp.stack([jnp.int32(v) for place in places for v in place]), tokens, *pieces)


def hidden_kernel(maps_ref, tokens_ref, out_ref):
    out_ref[...] = dot(maps_ref[...], tokens_ref[...], ((1,), (1,)))


def hidden_product(maps, tokens):
    rows, depth = tokens.shape
    tile = rows // 4
    return pl.pallas_call(
        hidden_kernel,
        out_shape=jax.ShapeDtypeStruct((maps.shape[0], rows), jnp.float32),
        grid=(rows // tile,),
        in_specs=[
            pl.BlockSpec(maps.shape, lambda i: (0, 0)),
            pl.BlockSpec((tile, depth), lambda i: (i, 0)),
        ],
        out_specs=pl.BlockSpec((maps.shape[0], tile), lambda i: (0, i)),
        compiler_params=pltpu.CompilerParams(vmem_limit_bytes=VMEM_BYTES),
        cost_estimate=LITTLE,
        name="hidden_product",
    )(maps, tokens)


def term_kernel(space_ref, tokens_ref, out_ref):
    total = jnp.dot(space_ref[...], tokens_ref[...], preferred_element_type=jnp.float32)
    out_ref[...] = (ADAPTER_SCALING * total).astype(jnp.bfloat16)


def gradient_term(space, values):
    rows, depth = values.shape
    tile = depth // 8
    return pl.pallas_call(
        term_kernel,
        out_shape=jax.ShapeDtypeStruct((space.shape[0], depth), jnp.bfloat16),
        grid=(depth // tile,),
        in_specs=[
            pl.BlockSpec(space.shape, lambda i: (0, 0)),
            pl.BlockSpec((rows, tile), lambda i: (0, i)),
        ],
        out_specs=pl.BlockSpec((space.shape[0], tile), lambda i: (0, i)),
        compiler_params=pltpu.CompilerParams(vmem_limit_bytes=VMEM_BYTES),
        cost_estimate=LITTLE,
        name="gradient_term",
    )(space, values)


class Adapters:
    def __init__(self, tokens, adapt_a, adapt_b, cotangent, row_tenant, adapter_slot):
        self.tokens, self.cotangent = tokens, cotangent
        self.rows = tokens.shape[0]
        self.ten_dev, self.rank, _ = adapt_a.shape
        self.peers, self.place = lax.axis_size("dp"), lax.axis_index("dp")
        tenants_all, blocks = adapter_slot.shape[0], self.rows // BLOCK
        first = row_tenant.reshape(blocks, BLOCK)[:, 0]
        table_ids = jnp.arange(tenants_all, dtype=jnp.int32)
        block_slot = jnp.sum(
            jnp.where(first[:, None] == table_ids[None, :], adapter_slot[None, :], 0), axis=1
        )
        block_home = block_slot // self.ten_dev
        block_local = block_slot % self.ten_dev
        peer_ids = jnp.arange(self.peers, dtype=jnp.int32)
        match = block_home[:, None] == peer_ids[None, :]
        self.wanted = self.ten_dev + jnp.sum(
            jnp.where(match, (block_local - self.ten_dev)[:, None], 0), axis=0
        )
        columns = self.peers * self.rank
        row_home = jnp.broadcast_to(block_home[:, None], (blocks, BLOCK)).reshape(1, -1)
        home_of = lax.broadcasted_iota(jnp.int32, (columns, self.rows), 0) // self.rank
        self.counted = (row_home == home_of) & (row_tenant != tenants_all)[None, :]
        output_columns = cotangent.shape[1]
        column = lax.axis_index("tensor") * output_columns
        self.own_a = adapt_a
        self.own_b = lax.dynamic_slice_in_dim(adapt_b, column, output_columns, 2)

    def exchange(self, sent):
        return lax.all_to_all(
            sent.reshape(self.peers, -1, sent.shape[1]), "dp", split_axis=0, concat_axis=0, tiled=True
        ).reshape(sent.shape)

    def choose(self, asked):
        asked_rows = jnp.broadcast_to(asked, (self.peers, self.rank)).reshape(-1, 1)
        shape = (self.peers * self.rank, self.ten_dev * self.rank)
        out_row = lax.broadcasted_iota(jnp.int32, shape, 0)
        slot_row = lax.broadcasted_iota(jnp.int32, shape, 1)
        self.select = (
            (asked_rows == slot_row // self.rank) & (out_row % self.rank == slot_row % self.rank)
        ).astype(jnp.bfloat16)

    def chosen(self, table):
        return dot(
            self.select, table.reshape(self.ten_dev * self.rank, -1), ((1,), (0,))
        ).astype(jnp.bfloat16)

    def rank_space(self, part):
        total = part + lax.ppermute(part, "tensor", SWAP)
        return jnp.where(self.counted, total, 0.0).astype(jnp.bfloat16)

    def term(self, space, values):
        return (ADAPTER_SCALING * dot(space, values, ((1,), (0,)))).astype(jnp.bfloat16)

    def total(self, came):
        return (
            dot(self.select, came, ((0,), (0,)))
            .astype(jnp.bfloat16)
            .reshape(self.ten_dev, self.rank, -1)
        )


def plain(tokens, base_weight, adapters):
    adapters.choose(adapters.exchange(adapters.wanted.reshape(-1, 1)))
    full = jnp.dot(
        tokens,
        lax.all_gather(base_weight, "dp", axis=1, tiled=True),
        preferred_element_type=jnp.float32,
    )
    base = lax.psum_scatter(full, "tensor", scatter_dimension=1, tiled=True)
    got_b = adapters.exchange(adapters.chosen(adapters.own_b))
    got_a = adapters.exchange(adapters.chosen(adapters.own_a))
    backward_pass = adapters.rank_space(dot(got_b, adapters.cotangent, ((1,), (1,))))
    came_a = adapters.exchange(adapters.term(backward_pass, tokens))
    hidden = adapters.rank_space(dot(got_a, tokens, ((1,), (1,))))
    came_b = adapters.exchange(adapters.term(hidden, adapters.cotangent))
    added = ADAPTER_SCALING * dot(hidden, got_b, ((0,), (0,)))
    return (
        (base + added).astype(jnp.bfloat16),
        adapters.total(came_a),
        adapters.total(came_b),
    )


def shards(tokens, base_weight, adapt_a, adapt_b, cotangent, row_tenant, adapter_slot):
    work = Adapters(tokens, adapt_a, adapt_b, cotangent, row_tenant, adapter_slot)
    if lax.axis_size("dp") != 8 or lax.axis_size("groups") != 2:
        return plain(tokens, base_weight, work)
    width = base_weight.shape[0]
    place, group, core = lax.axis_index("dp"), lax.axis_index("groups"), lax.axis_index("tensor")
    layer, side = place // 2, place % 2
    inner = (layer == 1) | (layer == 2)
    pair = [(i, i ^ 2) for i in range(8)]
    middle = [(2, 4), (3, 5), (4, 2), (5, 3)]
    outward = [(2, 0), (3, 1), (4, 6), (5, 7)]
    across = [(i, i ^ 1) for i in range(8)]

    def over(part, pairs):
        return lax.ppermute(part, "dp", pairs)

    def twin(part):
        return lax.ppermute(part, "groups", SWAP)

    output_columns = cotangent.shape[1]
    barrier = lax.optimization_barrier

    half = lax.dynamic_slice_in_dim(base_weight, group * (width // 2), width // 2, 0)
    near = over(half, pair)
    mid_next = over(half, middle)
    own_across = over(half, across)
    asked = work.exchange(work.wanted.reshape(-1, 1))
    near, mid_next, own_across, asked = barrier((near, mid_next, own_across, asked))
    mid_far = over(near, middle)
    end_next = over(mid_next, outward)
    near_across = over(near, across)
    near_rest = twin(near)
    own_across_rest = twin(own_across)
    work.choose(asked)
    got_b = work.exchange(work.chosen(work.own_b))
    send_a = work.chosen(work.own_a)
    mid_far, end_next, near_across, near_rest, own_across_rest, got_b, send_a = barrier(
        (mid_far, end_next, near_across, near_rest, own_across_rest, got_b, send_a)
    )
    got_a = work.exchange(send_a)
    end_far = over(mid_far, outward)
    following = jnp.where(inner, mid_next, end_next)
    following_across = over(following, across)
    following_rest = twin(following)
    near_across_rest = twin(near_across)
    backward_pass = work.rank_space(dot(got_b, cotangent, ((1,), (1,))))
    home_a = gradient_term(backward_pass, tokens)
    end_far, home_a = barrier((end_far, home_a))
    far = jnp.where(inner, mid_far, end_far)
    (
        got_a,
        home_a,
        far,
        following_across,
        following_rest,
        near_across_rest,
    ) = barrier(
        (
            got_a,
            home_a,
            far,
            following_across,
            following_rest,
            near_across_rest,
        )
    )
    came_a = work.exchange(home_a)
    far_across = over(far, across)
    far_rest = twin(far)
    following_across_rest = twin(following_across)
    parity = layer % 2
    product_here = product(
        tokens,
        [
            base_weight,
            own_across,
            own_across_rest,
            near,
            near_rest,
            near_across,
            near_across_rest,
        ],
        [
            (0, 2 * parity + side),
            (group, 2 * parity + 1 - side),
            (1 - group, 2 * parity + 1 - side),
            (group, 2 * (1 - parity) + side),
            (1 - group, 2 * (1 - parity) + side),
            (group, 2 * (1 - parity) + 1 - side),
            (1 - group, 2 * (1 - parity) + 1 - side),
        ],
        output_columns,
        cost(*tokens.shape, output_columns),
    )
    got_a, product_here, far_rest, far_across, following_across_rest = barrier(
        (got_a, product_here, far_rest, far_across, following_across_rest)
    )
    far_across_rest = twin(far_across)
    halves = [
        product(
            tokens,
            list(pieces),
            [(row, column) for column in (side, 1 - side) for row in (group, 1 - group)],
            output_columns // 2,
            LITTLE,
        )
        for pieces in (
            (following, following_rest, following_across, following_across_rest),
            (far, far_rest, far_across, far_across_rest),
        )
    ]
    product_there = jnp.where(
        layer < 2, jnp.concatenate(halves, 1), jnp.concatenate(halves[::-1], 1)
    )
    hidden = work.rank_space(hidden_product(got_a, tokens))
    home_b = work.term(hidden, cotangent)
    added = ADAPTER_SCALING * dot(hidden, got_b, ((0,), (0,)))
    keep_here = layer // 2 == core
    keep = jnp.where(keep_here, product_here, product_there)
    give = jnp.where(keep_here, product_there, product_here)
    base = keep + lax.ppermute(give, "tensor", SWAP)
    proj_out = (base + added).astype(jnp.bfloat16)
    came_a, home_b, proj_out = barrier((came_a, home_b, proj_out))
    came_b = work.exchange(home_b)
    return proj_out, work.total(came_a), work.total(came_b)


def solution(mesh):
    return jax.shard_map(
        shards,
        mesh=mesh,
        in_specs=(
            P(("groups", "dp"), "tensor"),
            P("tensor", "dp"),
            P(("groups", "dp"), None, "tensor"),
            P(("groups", "dp"), None, None),
            P(("groups", "dp"), "tensor"),
            P(("groups", "dp")),
            P("groups"),
        ),
        out_specs=(
            P(("groups", "dp"), "tensor"),
            P(("groups", "dp"), None, "tensor"),
            P(("groups", "dp"), None, "tensor"),
        ),
        check_vma=False,
    )
```

```python
import functools

import jax
import jax.numpy as jnp
from jax import lax
from jax.experimental import pallas as pl
from jax.experimental.pallas import tpu as pltpu
from jax.sharding import PartitionSpec as P

BLOCK = 128


ADAPTER_SCALING = 2.0
SWAP = [(0, 1), (1, 0)]


def dot(left, right, contract):
    return lax.dot_general(
        left, right, ((contract[0], contract[1]), ((), ())), preferred_element_type=jnp.float32
    )


LITTLE = pl.CostEstimate(flops=1_000_000, bytes_accessed=10_000, transcendentals=0)


def cost(rows, depth, columns):
    return pl.CostEstimate(
        flops=2 * rows * depth * columns, bytes_accessed=2 * rows * depth, transcendentals=0
    )


VMEM_BYTES = 40 * 1024 * 1024


def product_kernel(count, place_ref, tokens_ref, *refs):
    pieces, out_ref, weight, sems = refs[:count], refs[count], refs[count + 1], refs[count + 2]

    @pl.when(pl.program_id(0) == 0)
    def _():
        copies = []
        for k, piece in enumerate(pieces):
            depth = piece.shape[0]
            row = pl.multiple_of(place_ref[2 * k] * depth, depth)
            column = pl.multiple_of(place_ref[2 * k + 1] * piece.shape[1], piece.shape[1])
            copies.append(
                pltpu.make_async_copy(
                    piece,
                    weight.at[pl.ds(row, depth), pl.ds(column, piece.shape[1])],
                    sems.at[k],
                )
            )
        for copy in copies:
            copy.start()
        for copy in copies:
            copy.wait()

    out_ref[...] = jnp.dot(tokens_ref[...], weight[...], preferred_element_type=jnp.float32)


def product(tokens, pieces, places, width, estimate, vmem=VMEM_BYTES):
    rows, depth = tokens.shape
    tile = rows // 4
    return pl.pallas_call(
        functools.partial(product_kernel, len(pieces)),
        out_shape=jax.ShapeDtypeStruct((rows, width), jnp.float32),
        grid_spec=pltpu.PrefetchScalarGridSpec(
            num_scalar_prefetch=1,
            grid=(rows // tile,),
            in_specs=[pl.BlockSpec((tile, depth), lambda i, place: (i, 0))]
            + [pl.BlockSpec(memory_space=pl.ANY)] * len(pieces),
            out_specs=pl.BlockSpec((tile, width), lambda i, place: (i, 0)),
            scratch_shapes=[
                pltpu.VMEM((depth, width), jnp.bfloat16),
                pltpu.SemaphoreType.DMA((len(pieces),)),
            ],
        ),
        compiler_params=pltpu.CompilerParams(vmem_limit_bytes=vmem),
        cost_estimate=estimate,
        name="weight_product",
    )(jnp.stack([jnp.int32(v) for place in places for v in place]), tokens, *pieces)


def hidden_kernel(maps_ref, tokens_ref, out_ref):
    out_ref[...] = dot(maps_ref[...], tokens_ref[...], ((1,), (1,)))


def hidden_product(maps, tokens):
    rows, depth = tokens.shape
    tile = rows // 4
    return pl.pallas_call(
        hidden_kernel,
        out_shape=jax.ShapeDtypeStruct((maps.shape[0], rows), jnp.float32),
        grid=(rows // tile,),
        in_specs=[
            pl.BlockSpec(maps.shape, lambda i: (0, 0)),
            pl.BlockSpec((tile, depth), lambda i: (i, 0)),
        ],
        out_specs=pl.BlockSpec((maps.shape[0], tile), lambda i: (0, i)),
        compiler_params=pltpu.CompilerParams(vmem_limit_bytes=VMEM_BYTES),
        cost_estimate=LITTLE,
        name="hidden_product",
    )(maps, tokens)


def term_kernel(space_ref, tokens_ref, out_ref):
    total = jnp.dot(space_ref[...], tokens_ref[...], preferred_element_type=jnp.float32)
    out_ref[...] = (ADAPTER_SCALING * total).astype(jnp.bfloat16)


def gradient_term(space, values):
    rows, depth = values.shape
    tile = depth // 8
    return pl.pallas_call(
        term_kernel,
        out_shape=jax.ShapeDtypeStruct((space.shape[0], depth), jnp.bfloat16),
        grid=(depth // tile,),
        in_specs=[
            pl.BlockSpec(space.shape, lambda i: (0, 0)),
            pl.BlockSpec((rows, tile), lambda i: (0, i)),
        ],
        out_specs=pl.BlockSpec((space.shape[0], tile), lambda i: (0, i)),
        compiler_params=pltpu.CompilerParams(vmem_limit_bytes=VMEM_BYTES),
        cost_estimate=LITTLE,
        name="gradient_term",
    )(space, values)


class Adapters:
    def __init__(self, tokens, adapt_a, adapt_b, cotangent, row_tenant, adapter_slot):
        self.tokens, self.cotangent = tokens, cotangent
        self.rows = tokens.shape[0]
        self.ten_dev, self.rank, _ = adapt_a.shape
        self.peers, self.place = lax.axis_size("dp"), lax.axis_index("dp")
        tenants_all, blocks = adapter_slot.shape[0], self.rows // BLOCK
        first = row_tenant.reshape(blocks, BLOCK)[:, 0]
        table_ids = jnp.arange(tenants_all, dtype=jnp.int32)
        block_slot = jnp.sum(
            jnp.where(first[:, None] == table_ids[None, :], adapter_slot[None, :], 0), axis=1
        )
        block_home = block_slot // self.ten_dev
        block_local = block_slot % self.ten_dev
        peer_ids = jnp.arange(self.peers, dtype=jnp.int32)
        match = block_home[:, None] == peer_ids[None, :]
        self.wanted = self.ten_dev + jnp.sum(
            jnp.where(match, (block_local - self.ten_dev)[:, None], 0), axis=0
        )
        columns = self.peers * self.rank
        row_home = jnp.broadcast_to(block_home[:, None], (blocks, BLOCK)).reshape(1, -1)
        home_of = lax.broadcasted_iota(jnp.int32, (columns, self.rows), 0) // self.rank
        self.counted = (row_home == home_of) & (row_tenant != tenants_all)[None, :]
        output_columns = cotangent.shape[1]
        column = lax.axis_index("tensor") * output_columns
        self.own_a = adapt_a
        self.own_b = lax.dynamic_slice_in_dim(adapt_b, column, output_columns, 2)

    def exchange(self, sent):
        return lax.all_to_all(
            sent.reshape(self.peers, -1, sent.shape[1]), "dp", split_axis=0, concat_axis=0, tiled=True
        ).reshape(sent.shape)

    def choose(self, asked):
        asked_rows = jnp.broadcast_to(asked, (self.peers, self.rank)).reshape(-1, 1)
        shape = (self.peers * self.rank, self.ten_dev * self.rank)
        out_row = lax.broadcasted_iota(jnp.int32, shape, 0)
        slot_row = lax.broadcasted_iota(jnp.int32, shape, 1)
        self.select = (
            (asked_rows == slot_row // self.rank) & (out_row % self.rank == slot_row % self.rank)
        ).astype(jnp.bfloat16)

    def chosen(self, table):
        return dot(
            self.select, table.reshape(self.ten_dev * self.rank, -1), ((1,), (0,))
        ).astype(jnp.bfloat16)

    def rank_space(self, part):
        total = part + lax.ppermute(part, "tensor", SWAP)
        return jnp.where(self.counted, total, 0.0).astype(jnp.bfloat16)

    def term(self, space, values):
        return (ADAPTER_SCALING * dot(space, values, ((1,), (0,)))).astype(jnp.bfloat16)

    def total(self, came):
        return (
            dot(self.select, came, ((0,), (0,)))
            .astype(jnp.bfloat16)
            .reshape(self.ten_dev, self.rank, -1)
        )


def plain(tokens, base_weight, adapters):
    adapters.choose(adapters.exchange(adapters.wanted.reshape(-1, 1)))
    full = jnp.dot(
        tokens,
        lax.all_gather(base_weight, "dp", axis=1, tiled=True),
        preferred_element_type=jnp.float32,
    )
    base = lax.psum_scatter(full, "tensor", scatter_dimension=1, tiled=True)
    got_b = adapters.exchange(adapters.chosen(adapters.own_b))
    got_a = adapters.exchange(adapters.chosen(adapters.own_a))
    backward_pass = adapters.rank_space(dot(got_b, adapters.cotangent, ((1,), (1,))))
    came_a = adapters.exchange(adapters.term(backward_pass, tokens))
    hidden = adapters.rank_space(dot(got_a, tokens, ((1,), (1,))))
    came_b = adapters.exchange(adapters.term(hidden, adapters.cotangent))
    added = ADAPTER_SCALING * dot(hidden, got_b, ((0,), (0,)))
    return (
        (base + added).astype(jnp.bfloat16),
        adapters.total(came_a),
        adapters.total(came_b),
    )


def shards(tokens, base_weight, adapt_a, adapt_b, cotangent, row_tenant, adapter_slot):
    work = Adapters(tokens, adapt_a, adapt_b, cotangent, row_tenant, adapter_slot)
    if lax.axis_size("dp") != 8 or lax.axis_size("groups") != 2:
        return plain(tokens, base_weight, work)
    width = base_weight.shape[0]
    place, group, core = lax.axis_index("dp"), lax.axis_index("groups"), lax.axis_index("tensor")
    layer, side = place // 2, place % 2
    inner = (layer == 1) | (layer == 2)
    pair = [(i, i ^ 2) for i in range(8)]
    middle = [(2, 4), (3, 5), (4, 2), (5, 3)]
    outward = [(2, 0), (3, 1), (4, 6), (5, 7)]
    across = [(i, i ^ 1) for i in range(8)]

    def over(part, pairs):
        return lax.ppermute(part, "dp", pairs)

    def twin(part):
        return lax.ppermute(part, "groups", SWAP)

    output_columns = cotangent.shape[1]
    barrier = lax.optimization_barrier

    half = lax.dynamic_slice_in_dim(base_weight, group * (width // 2), width // 2, 0)
    near = over(half, pair)
    mid_next = over(half, middle)
    own_across = over(half, across)
    asked = work.exchange(work.wanted.reshape(-1, 1))
    near, mid_next = barrier((near, mid_next))
    mid_far = over(near, middle)
    end_next = over(mid_next, outward)
    near_across = over(near, across)
    near_rest = twin(near)
    work.choose(asked)
    got_b = work.exchange(work.chosen(work.own_b))
    own_a, own_across, near_rest, near_across, mid_far, end_next = barrier(
        (work.own_a, own_across, near_rest, near_across, mid_far, end_next)
    )
    send_a = work.chosen(own_a)
    got_b, send_a = barrier((got_b, send_a))
    got_a = work.exchange(send_a)
    end_far = over(mid_far, outward)
    following = jnp.where(inner, mid_next, end_next)
    following_across = over(following, across)
    following_rest = twin(following)
    near_across_rest = twin(near_across)
    own_across_rest = twin(own_across)
    backward_pass = work.rank_space(dot(got_b, cotangent, ((1,), (1,))))
    home_a = gradient_term(backward_pass, tokens)
    end_far, home_a = barrier((end_far, home_a))
    far = jnp.where(inner, mid_far, end_far)
    (
        got_a,
        home_a,
        far,
        following_across,
        following_rest,
        near_across_rest,
        own_across_rest,
    ) = barrier(
        (
            got_a,
            home_a,
            far,
            following_across,
            following_rest,
            near_across_rest,
            own_across_rest,
        )
    )
    came_a = work.exchange(home_a)
    far_across = over(far, across)
    far_rest = twin(far)
    following_across_rest = twin(following_across)
    parity = layer % 2
    product_here = product(
        tokens,
        [
            base_weight,
            own_across,
            own_across_rest,
            near,
            near_rest,
            near_across,
            near_across_rest,
        ],
        [
            (0, 2 * parity + side),
            (group, 2 * parity + 1 - side),
            (1 - group, 2 * parity + 1 - side),
            (group, 2 * (1 - parity) + side),
            (1 - group, 2 * (1 - parity) + side),
            (group, 2 * (1 - parity) + 1 - side),
            (1 - group, 2 * (1 - parity) + 1 - side),
        ],
        output_columns,
        cost(*tokens.shape, output_columns),
        56 * 1024 * 1024,
    )
    got_a, product_here, far_rest, following_across_rest, far_across = barrier(
        (got_a, product_here, far_rest, following_across_rest, far_across)
    )
    far_across_rest = twin(far_across)
    halves = [
        product(
            tokens,
            list(pieces),
            [(row, column) for column in (side, 1 - side) for row in (group, 1 - group)],
            output_columns // 2,
            LITTLE,
        )
        for pieces in (
            (following, following_rest, following_across, following_across_rest),
            (far, far_rest, far_across, far_across_rest),
        )
    ]
    product_there = jnp.where(
        layer < 2, jnp.concatenate(halves, 1), jnp.concatenate(halves[::-1], 1)
    )
    hidden = work.rank_space(hidden_product(got_a, tokens))
    home_b = work.term(hidden, cotangent)
    added = ADAPTER_SCALING * dot(hidden, got_b, ((0,), (0,)))
    keep_here = layer // 2 == core
    keep = jnp.where(keep_here, product_here, product_there)
    give = jnp.where(keep_here, product_there, product_here)
    base = keep + lax.ppermute(give, "tensor", SWAP)
    proj_out = (base + added).astype(jnp.bfloat16)
    came_a, home_b, proj_out = barrier((came_a, home_b, proj_out))
    came_b = work.exchange(home_b)
    return proj_out, work.total(came_a), work.total(came_b)


def solution(mesh):
    return jax.shard_map(
        shards,
        mesh=mesh,
        in_specs=(
            P(("groups", "dp"), "tensor"),
            P("tensor", "dp"),
            P(("groups", "dp"), None, "tensor"),
            P(("groups", "dp"), None, None),
            P(("groups", "dp"), "tensor"),
            P(("groups", "dp")),
            P("groups"),
        ),
        out_specs=(
            P(("groups", "dp"), "tensor"),
            P(("groups", "dp"), None, "tensor"),
            P(("groups", "dp"), None, "tensor"),
        ),
        check_vma=False,
    )
```

```python
import functools

import jax
import jax.numpy as jnp
from jax import lax
from jax.experimental import pallas as pl
from jax.experimental.pallas import tpu as pltpu
from jax.sharding import PartitionSpec as P

BLOCK = 128


ADAPTER_SCALING = 2.0
SWAP = [(0, 1), (1, 0)]


def dot(left, right, contract):
    return lax.dot_general(
        left, right, ((contract[0], contract[1]), ((), ())), preferred_element_type=jnp.float32
    )


LITTLE = pl.CostEstimate(flops=1_000_000, bytes_accessed=10_000, transcendentals=0)


def cost(rows, depth, columns):
    return pl.CostEstimate(
        flops=2 * rows * depth * columns, bytes_accessed=2 * rows * depth, transcendentals=0
    )


VMEM_BYTES = 40 * 1024 * 1024


def product_kernel(count, place_ref, tokens_ref, *refs):
    pieces, out_ref, weight, sems = refs[:count], refs[count], refs[count + 1], refs[count + 2]

    @pl.when(pl.program_id(0) == 0)
    def _():
        copies = []
        for k, piece in enumerate(pieces):
            depth = piece.shape[0]
            row = pl.multiple_of(place_ref[2 * k] * depth, depth)
            column = pl.multiple_of(place_ref[2 * k + 1] * piece.shape[1], piece.shape[1])
            copies.append(
                pltpu.make_async_copy(
                    piece,
                    weight.at[pl.ds(row, depth), pl.ds(column, piece.shape[1])],
                    sems.at[k],
                )
            )
        for copy in copies:
            copy.start()
        for copy in copies:
            copy.wait()

    out_ref[...] = jnp.dot(tokens_ref[...], weight[...], preferred_element_type=jnp.float32)


def flat(places):
    return jnp.stack([jnp.int32(v) for place in places for v in place])


def product(tokens, pieces, places, width, estimate, vmem=VMEM_BYTES):
    rows, depth = tokens.shape
    tile = rows // 4
    return pl.pallas_call(
        functools.partial(product_kernel, len(pieces)),
        out_shape=jax.ShapeDtypeStruct((rows, width), jnp.float32),
        grid_spec=pltpu.PrefetchScalarGridSpec(
            num_scalar_prefetch=1,
            grid=(rows // tile,),
            in_specs=[pl.BlockSpec((tile, depth), lambda i, place: (i, 0))]
            + [pl.BlockSpec(memory_space=pl.ANY)] * len(pieces),
            out_specs=pl.BlockSpec((tile, width), lambda i, place: (i, 0)),
            scratch_shapes=[
                pltpu.VMEM((depth, width), jnp.bfloat16),
                pltpu.SemaphoreType.DMA((len(pieces),)),
            ],
        ),
        compiler_params=pltpu.CompilerParams(vmem_limit_bytes=vmem),
        cost_estimate=estimate,
        name="weight_product",
    )(places, tokens, *pieces)


def hidden_kernel(maps_ref, tokens_ref, out_ref):
    out_ref[...] = dot(maps_ref[...], tokens_ref[...], ((1,), (1,)))


def hidden_product(maps, tokens):
    rows, depth = tokens.shape
    tile = rows // 4
    return pl.pallas_call(
        hidden_kernel,
        out_shape=jax.ShapeDtypeStruct((maps.shape[0], rows), jnp.float32),
        grid=(rows // tile,),
        in_specs=[
            pl.BlockSpec(maps.shape, lambda i: (0, 0)),
            pl.BlockSpec((tile, depth), lambda i: (i, 0)),
        ],
        out_specs=pl.BlockSpec((maps.shape[0], tile), lambda i: (0, i)),
        compiler_params=pltpu.CompilerParams(vmem_limit_bytes=VMEM_BYTES),
        cost_estimate=LITTLE,
        name="hidden_product",
    )(maps, tokens)


def term_kernel(space_ref, tokens_ref, out_ref):
    total = jnp.dot(space_ref[...], tokens_ref[...], preferred_element_type=jnp.float32)
    out_ref[...] = (ADAPTER_SCALING * total).astype(jnp.bfloat16)


def gradient_term(space, values):
    rows, depth = values.shape
    tile = depth // 8
    return pl.pallas_call(
        term_kernel,
        out_shape=jax.ShapeDtypeStruct((space.shape[0], depth), jnp.bfloat16),
        grid=(depth // tile,),
        in_specs=[
            pl.BlockSpec(space.shape, lambda i: (0, 0)),
            pl.BlockSpec((rows, tile), lambda i: (0, i)),
        ],
        out_specs=pl.BlockSpec((space.shape[0], tile), lambda i: (0, i)),
        compiler_params=pltpu.CompilerParams(vmem_limit_bytes=VMEM_BYTES),
        cost_estimate=LITTLE,
        name="gradient_term",
    )(space, values)


class Adapters:
    def __init__(self, tokens, adapt_a, adapt_b, cotangent, row_tenant, adapter_slot):
        self.tokens, self.cotangent = tokens, cotangent
        self.rows = tokens.shape[0]
        self.ten_dev, self.rank, _ = adapt_a.shape
        self.peers, self.place = lax.axis_size("dp"), lax.axis_index("dp")
        tenants_all, blocks = adapter_slot.shape[0], self.rows // BLOCK
        first = row_tenant.reshape(blocks, BLOCK)[:, 0]
        table_ids = jnp.arange(tenants_all, dtype=jnp.int32)
        block_slot = jnp.sum(
            jnp.where(first[:, None] == table_ids[None, :], adapter_slot[None, :], 0), axis=1
        )
        block_home = block_slot // self.ten_dev
        block_local = block_slot % self.ten_dev
        peer_ids = jnp.arange(self.peers, dtype=jnp.int32)
        match = block_home[:, None] == peer_ids[None, :]
        self.wanted = self.ten_dev + jnp.sum(
            jnp.where(match, (block_local - self.ten_dev)[:, None], 0), axis=0
        )
        columns = self.peers * self.rank
        row_home = jnp.broadcast_to(block_home[:, None], (blocks, BLOCK)).reshape(1, -1)
        home_of = lax.broadcasted_iota(jnp.int32, (columns, self.rows), 0) // self.rank
        self.counted = (row_home == home_of) & (row_tenant != tenants_all)[None, :]
        output_columns = cotangent.shape[1]
        column = lax.axis_index("tensor") * output_columns
        self.own_a = adapt_a
        self.own_b = lax.dynamic_slice_in_dim(adapt_b, column, output_columns, 2)

    def exchange(self, sent):
        return lax.all_to_all(
            sent.reshape(self.peers, -1, sent.shape[1]), "dp", split_axis=0, concat_axis=0, tiled=True
        ).reshape(sent.shape)

    def choose(self, asked):
        asked_rows = jnp.broadcast_to(asked, (self.peers, self.rank)).reshape(-1, 1)
        shape = (self.peers * self.rank, self.ten_dev * self.rank)
        out_row = lax.broadcasted_iota(jnp.int32, shape, 0)
        slot_row = lax.broadcasted_iota(jnp.int32, shape, 1)
        self.select = (
            (asked_rows == slot_row // self.rank) & (out_row % self.rank == slot_row % self.rank)
        ).astype(jnp.bfloat16)

    def chosen(self, table):
        return dot(
            self.select, table.reshape(self.ten_dev * self.rank, -1), ((1,), (0,))
        ).astype(jnp.bfloat16)

    def rank_space(self, part):
        total = part + lax.ppermute(part, "tensor", SWAP)
        return jnp.where(self.counted, total, 0.0).astype(jnp.bfloat16)

    def term(self, space, values):
        return (ADAPTER_SCALING * dot(space, values, ((1,), (0,)))).astype(jnp.bfloat16)

    def total(self, came):
        return (
            dot(self.select, came, ((0,), (0,)))
            .astype(jnp.bfloat16)
            .reshape(self.ten_dev, self.rank, -1)
        )


def plain(tokens, base_weight, adapters):
    adapters.choose(adapters.exchange(adapters.wanted.reshape(-1, 1)))
    full = jnp.dot(
        tokens,
        lax.all_gather(base_weight, "dp", axis=1, tiled=True),
        preferred_element_type=jnp.float32,
    )
    base = lax.psum_scatter(full, "tensor", scatter_dimension=1, tiled=True)
    got_b = adapters.exchange(adapters.chosen(adapters.own_b))
    got_a = adapters.exchange(adapters.chosen(adapters.own_a))
    backward_pass = adapters.rank_space(dot(got_b, adapters.cotangent, ((1,), (1,))))
    came_a = adapters.exchange(adapters.term(backward_pass, tokens))
    hidden = adapters.rank_space(dot(got_a, tokens, ((1,), (1,))))
    came_b = adapters.exchange(adapters.term(hidden, adapters.cotangent))
    added = ADAPTER_SCALING * dot(hidden, got_b, ((0,), (0,)))
    return (
        (base + added).astype(jnp.bfloat16),
        adapters.total(came_a),
        adapters.total(came_b),
    )


def shards(tokens, base_weight, adapt_a, adapt_b, cotangent, row_tenant, adapter_slot):
    work = Adapters(tokens, adapt_a, adapt_b, cotangent, row_tenant, adapter_slot)
    if lax.axis_size("dp") != 8 or lax.axis_size("groups") != 2:
        return plain(tokens, base_weight, work)
    width = base_weight.shape[0]
    place, group, core = lax.axis_index("dp"), lax.axis_index("groups"), lax.axis_index("tensor")
    layer, side = place // 2, place % 2
    inner = (layer == 1) | (layer == 2)
    pair = [(i, i ^ 2) for i in range(8)]
    middle = [(2, 4), (3, 5), (4, 2), (5, 3)]
    outward = [(2, 0), (3, 1), (4, 6), (5, 7)]
    across = [(i, i ^ 1) for i in range(8)]

    def over(part, pairs):
        return lax.ppermute(part, "dp", pairs)

    def twin(part):
        return lax.ppermute(part, "groups", SWAP)

    output_columns = cotangent.shape[1]
    barrier = lax.optimization_barrier

    parity = layer % 2
    places_here = flat(
        [(0, 2 * parity + side)]
        + [
            (row, column)
            for column in (
                2 * parity + 1 - side,
                2 * (1 - parity) + side,
                2 * (1 - parity) + 1 - side,
            )
            for row in (group, 1 - group)
        ]
    )
    places_half = flat([(row, column) for column in (side, 1 - side) for row in (group, 1 - group)])
    half = lax.dynamic_slice_in_dim(base_weight, group * (width // 2), width // 2, 0)
    near = over(half, pair)
    mid_next = over(half, middle)
    own_across = over(half, across)
    asked = work.exchange(work.wanted.reshape(-1, 1))
    near, mid_next, places_here, places_half = barrier((near, mid_next, places_here, places_half))
    mid_far = over(near, middle)
    end_next = over(mid_next, outward)
    near_across = over(near, across)
    near_rest = twin(near)
    work.choose(asked)
    got_b = work.exchange(work.chosen(work.own_b))
    own_a, own_across, near_rest, near_across, mid_far, end_next = barrier(
        (work.own_a, own_across, near_rest, near_across, mid_far, end_next)
    )
    send_a = work.chosen(own_a)
    got_b, send_a = barrier((got_b, send_a))
    got_a = work.exchange(send_a)
    end_far = over(mid_far, outward)
    following = jnp.where(inner, mid_next, end_next)
    following_across = over(following, across)
    following_rest = twin(following)
    near_across_rest = twin(near_across)
    own_across_rest = twin(own_across)
    backward_pass = work.rank_space(dot(got_b, cotangent, ((1,), (1,))))
    home_a = gradient_term(backward_pass, tokens)
    end_far, home_a, following_across = barrier((end_far, home_a, following_across))
    far = jnp.where(inner, mid_far, end_far)
    got_a, home_a, following_rest, near_across_rest, own_across_rest = barrier(
        (got_a, home_a, following_rest, near_across_rest, own_across_rest)
    )
    came_a = work.exchange(home_a)
    far_across = over(far, across)
    far_rest = twin(far)
    following_across_rest = twin(following_across)
    product_here = product(
        tokens,
        [
            base_weight,
            own_across,
            own_across_rest,
            near,
            near_rest,
            near_across,
            near_across_rest,
        ],
        places_here,
        output_columns,
        cost(*tokens.shape, output_columns),
        56 * 1024 * 1024,
    )
    got_a, product_here, far_rest, following_across_rest, far_across = barrier(
        (got_a, product_here, far_rest, following_across_rest, far_across)
    )
    far_across_rest = twin(far_across)
    halves = [
        product(
            tokens,
            list(pieces),
            places_half,
            output_columns // 2,
            LITTLE,
        )
        for pieces in (
            (following, following_rest, following_across, following_across_rest),
            (far, far_rest, far_across, far_across_rest),
        )
    ]
    product_there = jnp.where(
        layer < 2, jnp.concatenate(halves, 1), jnp.concatenate(halves[::-1], 1)
    )
    hidden = work.rank_space(hidden_product(got_a, tokens))
    home_b = work.term(hidden, cotangent)
    added = ADAPTER_SCALING * dot(hidden, got_b, ((0,), (0,)))
    keep_here = layer // 2 == core
    keep = jnp.where(keep_here, product_here, product_there)
    give = jnp.where(keep_here, product_there, product_here)
    base = keep + lax.ppermute(give, "tensor", SWAP)
    proj_out = (base + added).astype(jnp.bfloat16)
    came_a, home_b, proj_out = barrier((came_a, home_b, proj_out))
    came_b = work.exchange(home_b)
    return proj_out, work.total(came_a), work.total(came_b)


def solution(mesh):
    return jax.shard_map(
        shards,
        mesh=mesh,
        in_specs=(
            P(("groups", "dp"), "tensor"),
            P("tensor", "dp"),
            P(("groups", "dp"), None, "tensor"),
            P(("groups", "dp"), None, None),
            P(("groups", "dp"), "tensor"),
            P(("groups", "dp")),
            P("groups"),
        ),
        out_specs=(
            P(("groups", "dp"), "tensor"),
            P(("groups", "dp"), None, "tensor"),
            P(("groups", "dp"), None, "tensor"),
        ),
        check_vma=False,
    )
```

```python
import functools

import jax
import jax.numpy as jnp
from jax import lax
from jax.experimental import pallas as pl
from jax.experimental.pallas import tpu as pltpu
from jax.sharding import PartitionSpec as P

BLOCK = 128


ADAPTER_SCALING = 2.0
SWAP = [(0, 1), (1, 0)]


def dot(left, right, contract):
    return lax.dot_general(
        left, right, ((contract[0], contract[1]), ((), ())), preferred_element_type=jnp.float32
    )


LITTLE = pl.CostEstimate(flops=1_000_000, bytes_accessed=10_000, transcendentals=0)


def cost(rows, depth, columns):
    return pl.CostEstimate(
        flops=2 * rows * depth * columns, bytes_accessed=2 * rows * depth, transcendentals=0
    )


VMEM_BYTES = 40 * 1024 * 1024


def product_kernel(count, place_ref, tokens_ref, *refs):
    pieces, out_ref, weight, sems = refs[:count], refs[count], refs[count + 1], refs[count + 2]

    @pl.when(pl.program_id(0) == 0)
    def _():
        copies = []
        for k, piece in enumerate(pieces):
            depth = piece.shape[0]
            row = pl.multiple_of(place_ref[2 * k] * depth, depth)
            column = pl.multiple_of(place_ref[2 * k + 1] * piece.shape[1], piece.shape[1])
            copies.append(
                pltpu.make_async_copy(
                    piece,
                    weight.at[pl.ds(row, depth), pl.ds(column, piece.shape[1])],
                    sems.at[k],
                )
            )
        for copy in copies:
            copy.start()
        for copy in copies:
            copy.wait()

    out_ref[...] = jnp.dot(tokens_ref[...], weight[...], preferred_element_type=jnp.float32)


def flat(places):
    return jnp.stack([jnp.int32(v) for place in places for v in place])


def product(tokens, pieces, places, width, estimate, vmem=VMEM_BYTES):
    rows, depth = tokens.shape
    tile = rows // 4
    return pl.pallas_call(
        functools.partial(product_kernel, len(pieces)),
        out_shape=jax.ShapeDtypeStruct((rows, width), jnp.float32),
        grid_spec=pltpu.PrefetchScalarGridSpec(
            num_scalar_prefetch=1,
            grid=(rows // tile,),
            in_specs=[pl.BlockSpec((tile, depth), lambda i, place: (i, 0))]
            + [pl.BlockSpec(memory_space=pl.ANY)] * len(pieces),
            out_specs=pl.BlockSpec((tile, width), lambda i, place: (i, 0)),
            scratch_shapes=[
                pltpu.VMEM((depth, width), jnp.bfloat16),
                pltpu.SemaphoreType.DMA((len(pieces),)),
            ],
        ),
        compiler_params=pltpu.CompilerParams(vmem_limit_bytes=vmem),
        cost_estimate=estimate,
        name="weight_product",
    )(places, tokens, *pieces)


def hidden_kernel(maps_ref, tokens_ref, out_ref):
    out_ref[...] = dot(maps_ref[...], tokens_ref[...], ((1,), (1,)))


def hidden_product(maps, tokens):
    rows, depth = tokens.shape
    tile = rows // 4
    return pl.pallas_call(
        hidden_kernel,
        out_shape=jax.ShapeDtypeStruct((maps.shape[0], rows), jnp.float32),
        grid=(rows // tile,),
        in_specs=[
            pl.BlockSpec(maps.shape, lambda i: (0, 0)),
            pl.BlockSpec((tile, depth), lambda i: (i, 0)),
        ],
        out_specs=pl.BlockSpec((maps.shape[0], tile), lambda i: (0, i)),
        compiler_params=pltpu.CompilerParams(vmem_limit_bytes=VMEM_BYTES),
        cost_estimate=LITTLE,
        name="hidden_product",
    )(maps, tokens)


def term_kernel(space_ref, tokens_ref, out_ref):
    total = jnp.dot(space_ref[...], tokens_ref[...], preferred_element_type=jnp.float32)
    out_ref[...] = (ADAPTER_SCALING * total).astype(jnp.bfloat16)


def gradient_term(space, values):
    rows, depth = values.shape
    tile = depth // 8
    return pl.pallas_call(
        term_kernel,
        out_shape=jax.ShapeDtypeStruct((space.shape[0], depth), jnp.bfloat16),
        grid=(depth // tile,),
        in_specs=[
            pl.BlockSpec(space.shape, lambda i: (0, 0)),
            pl.BlockSpec((rows, tile), lambda i: (0, i)),
        ],
        out_specs=pl.BlockSpec((space.shape[0], tile), lambda i: (0, i)),
        compiler_params=pltpu.CompilerParams(vmem_limit_bytes=VMEM_BYTES),
        cost_estimate=LITTLE,
        name="gradient_term",
    )(space, values)


class Adapters:
    def __init__(self, tokens, adapt_a, adapt_b, cotangent, row_tenant, adapter_slot):
        self.tokens, self.cotangent = tokens, cotangent
        self.rows = tokens.shape[0]
        self.ten_dev, self.rank, _ = adapt_a.shape
        self.peers, self.place = lax.axis_size("dp"), lax.axis_index("dp")
        tenants_all, blocks = adapter_slot.shape[0], self.rows // BLOCK
        first = row_tenant.reshape(blocks, BLOCK)[:, 0]
        table_ids = jnp.arange(tenants_all, dtype=jnp.int32)
        block_slot = jnp.sum(
            jnp.where(first[:, None] == table_ids[None, :], adapter_slot[None, :], 0), axis=1
        )
        block_home = block_slot // self.ten_dev
        block_local = block_slot % self.ten_dev
        peer_ids = jnp.arange(self.peers, dtype=jnp.int32)
        match = block_home[:, None] == peer_ids[None, :]
        self.wanted = self.ten_dev + jnp.sum(
            jnp.where(match, (block_local - self.ten_dev)[:, None], 0), axis=0
        )
        columns = self.peers * self.rank
        row_home = jnp.broadcast_to(block_home[:, None], (blocks, BLOCK)).reshape(1, -1)
        home_of = lax.broadcasted_iota(jnp.int32, (columns, self.rows), 0) // self.rank
        self.counted = (row_home == home_of) & (row_tenant != tenants_all)[None, :]
        output_columns = cotangent.shape[1]
        column = lax.axis_index("tensor") * output_columns
        self.own_a = adapt_a
        self.own_b = lax.dynamic_slice_in_dim(adapt_b, column, output_columns, 2)

    def exchange(self, sent):
        return lax.all_to_all(
            sent.reshape(self.peers, -1, sent.shape[1]), "dp", split_axis=0, concat_axis=0, tiled=True
        ).reshape(sent.shape)

    def choose(self, asked):
        asked_rows = jnp.broadcast_to(asked, (self.peers, self.rank)).reshape(-1, 1)
        shape = (self.peers * self.rank, self.ten_dev * self.rank)
        out_row = lax.broadcasted_iota(jnp.int32, shape, 0)
        slot_row = lax.broadcasted_iota(jnp.int32, shape, 1)
        self.select = (
            (asked_rows == slot_row // self.rank) & (out_row % self.rank == slot_row % self.rank)
        ).astype(jnp.bfloat16)

    def chosen(self, table):
        return dot(
            self.select, table.reshape(self.ten_dev * self.rank, -1), ((1,), (0,))
        ).astype(jnp.bfloat16)

    def rank_space(self, part):
        total = part + lax.ppermute(part, "tensor", SWAP)
        return jnp.where(self.counted, total, 0.0).astype(jnp.bfloat16)

    def term(self, space, values):
        return (ADAPTER_SCALING * dot(space, values, ((1,), (0,)))).astype(jnp.bfloat16)

    def total(self, came):
        return (
            dot(self.select, came, ((0,), (0,)))
            .astype(jnp.bfloat16)
            .reshape(self.ten_dev, self.rank, -1)
        )


def plain(tokens, base_weight, adapters):
    adapters.choose(adapters.exchange(adapters.wanted.reshape(-1, 1)))
    full = jnp.dot(
        tokens,
        lax.all_gather(base_weight, "dp", axis=1, tiled=True),
        preferred_element_type=jnp.float32,
    )
    base = lax.psum_scatter(full, "tensor", scatter_dimension=1, tiled=True)
    got_b = adapters.exchange(adapters.chosen(adapters.own_b))
    got_a = adapters.exchange(adapters.chosen(adapters.own_a))
    backward_pass = adapters.rank_space(dot(got_b, adapters.cotangent, ((1,), (1,))))
    came_a = adapters.exchange(adapters.term(backward_pass, tokens))
    hidden = adapters.rank_space(dot(got_a, tokens, ((1,), (1,))))
    came_b = adapters.exchange(adapters.term(hidden, adapters.cotangent))
    added = ADAPTER_SCALING * dot(hidden, got_b, ((0,), (0,)))
    return (
        (base + added).astype(jnp.bfloat16),
        adapters.total(came_a),
        adapters.total(came_b),
    )


def shards(tokens, base_weight, adapt_a, adapt_b, cotangent, row_tenant, adapter_slot):
    work = Adapters(tokens, adapt_a, adapt_b, cotangent, row_tenant, adapter_slot)
    if lax.axis_size("dp") != 8 or lax.axis_size("groups") != 2:
        return plain(tokens, base_weight, work)
    width = base_weight.shape[0]
    place, group, core = lax.axis_index("dp"), lax.axis_index("groups"), lax.axis_index("tensor")
    layer, side = place // 2, place % 2
    inner = (layer == 1) | (layer == 2)
    pair = [(i, i ^ 2) for i in range(8)]
    middle = [(2, 4), (3, 5), (4, 2), (5, 3)]
    outward = [(2, 0), (3, 1), (4, 6), (5, 7)]
    across = [(i, i ^ 1) for i in range(8)]

    def over(part, pairs):
        return lax.ppermute(part, "dp", pairs)

    def twin(part):
        return lax.ppermute(part, "groups", SWAP)

    output_columns = cotangent.shape[1]
    barrier = lax.optimization_barrier

    parity = layer % 2
    places_here = flat(
        [(0, 2 * parity + side)]
        + [
            (row, column)
            for column in (
                2 * parity + 1 - side,
                2 * (1 - parity) + side,
                2 * (1 - parity) + 1 - side,
            )
            for row in (group, 1 - group)
        ]
    )
    places_half = flat([(row, column) for column in (side, 1 - side) for row in (group, 1 - group)])
    half = lax.dynamic_slice_in_dim(base_weight, group * (width // 2), width // 2, 0)
    near = over(half, pair)
    mid_next = over(half, middle)
    own_across = over(half, across)
    asked = work.exchange(work.wanted.reshape(-1, 1))
    near, mid_next, places_here, places_half = barrier((near, mid_next, places_here, places_half))
    mid_far = over(near, middle)
    end_next = over(mid_next, outward)
    near_across = over(near, across)
    near_rest = twin(near)
    work.choose(asked)
    got_b = work.exchange(work.chosen(work.own_b))
    own_a, own_across, near_rest, near_across, mid_far, end_next = barrier(
        (work.own_a, own_across, near_rest, near_across, mid_far, end_next)
    )
    send_a = work.chosen(own_a)
    got_b, send_a = barrier((got_b, send_a))
    got_a = work.exchange(send_a)
    end_far = over(mid_far, outward)
    following = jnp.where(inner, mid_next, end_next)
    following_across = over(following, across)
    following_rest = twin(following)
    near_across_rest = twin(near_across)
    own_across_rest = twin(own_across)
    backward_pass = work.rank_space(dot(got_b, cotangent, ((1,), (1,))))
    home_a = gradient_term(backward_pass, tokens)
    end_far, home_a, following_across, following_rest = barrier(
        (end_far, home_a, following_across, following_rest)
    )
    far = jnp.where(inner, mid_far, end_far)
    got_a, home_a = barrier((got_a, home_a))
    came_a = work.exchange(home_a)
    far_across = over(far, across)
    far_rest = twin(far)
    following_across_rest = twin(following_across)
    product_here = product(
        tokens,
        [
            base_weight,
            own_across,
            own_across_rest,
            near,
            near_rest,
            near_across,
            near_across_rest,
        ],
        places_here,
        output_columns,
        cost(*tokens.shape, output_columns),
        56 * 1024 * 1024,
    )
    got_a, product_here, far_rest, following_across_rest, far_across = barrier(
        (got_a, product_here, far_rest, following_across_rest, far_across)
    )
    far_across_rest = twin(far_across)
    halves = [
        product(
            tokens,
            list(pieces),
            places_half,
            output_columns // 2,
            LITTLE,
        )
        for pieces in (
            (following, following_rest, following_across, following_across_rest),
            (far, far_rest, far_across, far_across_rest),
        )
    ]
    product_there = jnp.where(
        layer < 2, jnp.concatenate(halves, 1), jnp.concatenate(halves[::-1], 1)
    )
    hidden = work.rank_space(hidden_product(got_a, tokens))
    home_b = work.term(hidden, cotangent)
    added = ADAPTER_SCALING * dot(hidden, got_b, ((0,), (0,)))
    keep_here = layer // 2 == core
    keep = jnp.where(keep_here, product_here, product_there)
    give = jnp.where(keep_here, product_there, product_here)
    base = keep + lax.ppermute(give, "tensor", SWAP)
    proj_out = (base + added).astype(jnp.bfloat16)
    came_a, home_b, proj_out = barrier((came_a, home_b, proj_out))
    came_b = work.exchange(home_b)
    return proj_out, work.total(came_a), work.total(came_b)


def solution(mesh):
    return jax.shard_map(
        shards,
        mesh=mesh,
        in_specs=(
            P(("groups", "dp"), "tensor"),
            P("tensor", "dp"),
            P(("groups", "dp"), None, "tensor"),
            P(("groups", "dp"), None, None),
            P(("groups", "dp"), "tensor"),
            P(("groups", "dp")),
            P("groups"),
        ),
        out_specs=(
            P(("groups", "dp"), "tensor"),
            P(("groups", "dp"), None, "tensor"),
            P(("groups", "dp"), None, "tensor"),
        ),
        check_vma=False,
    )
```
